32 devices in a mesh: dp: 16 (over z, x, core), seq: 2 (over y).
Axes of the slice: x: 2, y: 2, z: 4, core: 2. Of those that a mesh axis runs over, the one named last changes fastest.
Arguments:
- block_entry_tokens: bfloat16 [16, 1024, 1024], P('dp', 'seq'), may hold values from -6 to 6
- result_cotangent: bfloat16 [16, 1024, 1024], P('dp', 'seq'), may hold values from -6 to 6
- leading_scale_factor: bfloat16 [1024], P('dp'), may hold values from 0.5 to 1.5
- leading_bias_vector: bfloat16 [1024], P('dp'), may hold values from -3 to 3
- query_key_value_matrix: bfloat16 [1024, 3072], P('dp'), may hold values from -0.25 to 0.25
- query_key_value_bias: bfloat16 [3072], P('dp'), may hold values from -3 to 3
- attention_exit_matrix: bfloat16 [1024, 1024], P('dp'), may hold values from -0.75 to 0.75
- attention_exit_bias: bfloat16 [1024], P('dp'), may hold values from -3 to 3
- latter_scale_factor: bfloat16 [1024], P('dp'), may hold values from 0.5 to 1.5
- latter_bias_vector: bfloat16 [1024], P('dp'), may hold values from -3 to 3
- expand_projection_matrix: bfloat16 [1024, 4096], P('dp'), may hold values from -0.1875 to 0.1875
- expand_projection_offset: bfloat16 [4096], P('dp'), may hold values from -3 to 3
- contract_projection_matrix: bfloat16 [4096, 1024], P('dp'), may hold values from -0.09375 to 0.09375
- contract_projection_offset: bfloat16 [1024], P('dp'), may hold values from -3 to 3
Outputs:
- block_output: float32 [16, 1024, 1024], P('dp', 'seq')
- input_grad: float32 [16, 1024, 1024], P('dp', 'seq')
- prenorm_gain_gradient: float32 [1024], P('dp')
- prenorm_shift_gradient: float32 [1024], P('dp')
- qkvmatrix_grad: float32 [1024, 3072], P('dp')
- qkvshift_grad: float32 [3072], P('dp')
- outmatrix_grad: float32 [1024, 1024], P('dp')
- outshift_grad: float32 [1024], P('dp')
- midgain_grad: float32 [1024], P('dp')
- midshift_grad: float32 [1024], P('dp')
- upmatrix_grad: float32 [1024, 4096], P('dp')
- upshift_grad: float32 [4096], P('dp')
- downmatrix_grad: float32 [4096, 1024], P('dp')
- downshift_grad: float32 [1024], P('dp')
The draws below stay inside these ranges and needn't reach their ends.
All inputs are finite; a program needn't handle non-finite values.
Results may differ from the reference program's by a relative error of at most 0.019.
Values may be sent and summed in bfloat16 or wider, within the bound.
A program may use at most 192 MiB of HBM per device.

```python
import jax
import jax.numpy as jnp
from jax import lax

EMBED_DIMENSION = 1024
H = 16
HD = 64
FF = 4096
SEQ_LEN = 1024
BATCH = 16


def block_levels(rng, shape, cuts, smallest, top_value):
    loudness, own = 1.0, jax.random.fold_in(rng, 6)
    for axis_at, blocks in cuts:
        heights = jnp.exp(jax.random.uniform(jax.random.fold_in(own, axis_at), (blocks,), jnp.float32, smallest / len(cuts), top_value / len(cuts)))
        loudness = loudness * jnp.repeat(heights, shape[axis_at] // blocks).reshape([-1 if axis == axis_at else 1 for axis in range(len(shape))])
    return loudness


def normal_values(own_key, shape, deviation, limit, cuts=(), held_as=jnp.bfloat16):
    array = deviation * jax.random.normal(own_key, shape, jnp.float32)
    if cuts:
        array = array * block_levels(own_key, shape, cuts, -0.22, 0.18)
    return jnp.clip(array, -limit, limit).astype(held_as)


def setup_inputs(seed: int = 0) -> dict:
    key_list = jax.random.split(jax.random.key(seed), 15)
    block_entry_tokens = normal_values(key_list[0], (BATCH, SEQ_LEN, EMBED_DIMENSION), 1.0, 6.0, ((0, 16), (1, 2)))
    result_cotangent = normal_values(key_list[1], (BATCH, SEQ_LEN, EMBED_DIMENSION), 1.0, 6.0, ((0, 16), (1, 2)))
    leading_scale_factor = jnp.clip(1.0 + 0.1 * jax.random.normal(key_list[2], (EMBED_DIMENSION,), jnp.float32), 0.5, 1.5).astype(jnp.bfloat16)
    leading_bias_vector = normal_values(key_list[3], (EMBED_DIMENSION,), 0.5, 3.0, ((0, 16),))
    query_key_value_matrix = normal_values(key_list[4], (EMBED_DIMENSION, 3 * EMBED_DIMENSION), (EMBED_DIMENSION // 2) ** -0.5, 0.25, ((0, 16),))
    query_key_value_bias = normal_values(key_list[5], (3 * EMBED_DIMENSION,), 0.5, 3.0, ((0, 16),))
    attention_exit_matrix = normal_values(key_list[6], (EMBED_DIMENSION, EMBED_DIMENSION), (EMBED_DIMENSION // 16) ** -0.5, 0.75, ((0, 16),))
    attention_exit_bias = normal_values(key_list[7], (EMBED_DIMENSION,), 0.5, 3.0, ((0, 16),))
    latter_scale_factor = jnp.clip(1.0 + 0.1 * jax.random.normal(key_list[8], (EMBED_DIMENSION,), jnp.float32), 0.5, 1.5).astype(jnp.bfloat16)
    latter_bias_vector = normal_values(key_list[9], (EMBED_DIMENSION,), 0.5, 3.0, ((0, 16),))
    expand_projection_matrix = normal_values(key_list[10], (EMBED_DIMENSION, FF), EMBED_DIMENSION ** -0.5, 0.1875, ((0, 16),))
    expand_projection_offset = normal_values(key_list[11], (FF,), 0.5, 3.0, ((0, 16),))
    contract_projection_matrix = normal_values(key_list[12], (FF, EMBED_DIMENSION), FF ** -0.5, 0.09375, ((0, 16),))
    contract_projection_offset = normal_values(key_list[13], (EMBED_DIMENSION,), 0.5, 3.0, ((0, 16),))
    return dict(block_entry_tokens=block_entry_tokens, result_cotangent=result_cotangent, leading_scale_factor=leading_scale_factor, leading_bias_vector=leading_bias_vector, query_key_value_matrix=query_key_value_matrix, query_key_value_bias=query_key_value_bias, attention_exit_matrix=attention_exit_matrix, attention_exit_bias=attention_exit_bias, latter_scale_factor=latter_scale_factor, latter_bias_vector=latter_bias_vector, expand_projection_matrix=expand_projection_matrix, expand_projection_offset=expand_projection_offset, contract_projection_matrix=contract_projection_matrix, contract_projection_offset=contract_projection_offset)


@jax.custom_vjp
def low(v):
    return lax.optimization_barrier(v.astype(jnp.bfloat16)).astype(jnp.float32)

@jax.custom_vjp
def low_back(v):
    return v

def low_keep(v):
    return (low(v), None)

def low_pass(kept, grad):
    return (grad,)

def back_keep(v):
    return (v, None)

def back_low(kept, grad):
    return (low(grad),)
low.defvjp(low_keep, low_pass)
low_back.defvjp(back_keep, back_low)
EPS = 1e-05
NEG = -1e+30
HIGH = lax.Precision.HIGHEST

def standardize_features(values, gain, shift):
    center = values - lax.optimization_barrier(jnp.mean(values, -1, keepdims=True))
    spread = lax.optimization_barrier(jnp.mean(center * center, -1, keepdims=True))
    return center * lax.rsqrt(spread + EPS) * gain + shift

def causal_head(queries, keyset, values):
    factor = queries.shape[-1] ** (-0.5)
    scores = low_back(jnp.dot(queries, keyset.T, precision=HIGH) * factor)
    extent = scores.shape[0]
    query_pos = lax.broadcasted_iota(jnp.int32, (extent, extent), 0)
    key_pos = lax.broadcasted_iota(jnp.int32, (extent, extent), 1)
    scores = jnp.where(key_pos <= query_pos, scores, NEG)
    probab = jax.nn.softmax(scores, axis=-1)
    return jnp.dot(low(probab), values, precision=HIGH)

def head_group(group):
    return causal_head(group[0], group[1], group[2])

def evaluate_block(entering_tensors, leading_scale_factor, leading_bias_vector, query_key_value_matrix, query_key_value_bias, attention_exit_matrix, attention_exit_bias, latter_scale_factor, latter_bias_vector, expand_projection_matrix, expand_projection_offset, contract_projection_matrix, contract_projection_offset):
    length = entering_tensors.shape[0]
    standardized_tokens = low(standardize_features(entering_tensors, leading_scale_factor, leading_bias_vector))
    packed = low(low_back(jnp.dot(standardized_tokens, query_key_value_matrix, precision=HIGH) + query_key_value_bias))
    grouped = packed.reshape(length, 3, H, HD).transpose(2, 1, 0, 3)
    context = lax.map(jax.checkpoint(head_group), grouped)
    context = context.transpose(1, 0, 2).reshape(length, EMBED_DIMENSION)
    context = low_back(low(context))
    attended = low_back(jnp.dot(context, attention_exit_matrix, precision=HIGH) + attention_exit_bias)
    resid = entering_tensors + attended
    normed_two = low(standardize_features(resid, latter_scale_factor, latter_bias_vector))
    upact = low_back(jnp.dot(normed_two, expand_projection_matrix, precision=HIGH) + expand_projection_offset)
    activ = low(jax.nn.gelu(upact, approximate=True))
    downact = low_back(jnp.dot(activ, contract_projection_matrix, precision=HIGH) + contract_projection_offset)
    return resid + downact

def reference(block_entry_tokens, result_cotangent, leading_scale_factor, leading_bias_vector, query_key_value_matrix, query_key_value_bias, attention_exit_matrix, attention_exit_bias, latter_scale_factor, latter_bias_vector, expand_projection_matrix, expand_projection_offset, contract_projection_matrix, contract_projection_offset):
    block_weight_bundle = tuple((replica_place.astype(jnp.float32) for replica_place in (leading_scale_factor, leading_bias_vector, query_key_value_matrix, query_key_value_bias, attention_exit_matrix, attention_exit_bias, latter_scale_factor, latter_bias_vector, expand_projection_matrix, expand_projection_offset, contract_projection_matrix, contract_projection_offset)))

    def one_sequence(totals, pair):
        entering_tensors, cotangent = pair
        output, pullback = jax.vjp(evaluate_block, entering_tensors.astype(jnp.float32), *block_weight_bundle)
        grads = pullback(cotangent.astype(jnp.float32))
        totals = tuple((left + right for left, right in zip(totals, grads[1:])))
        return (totals, (output, grads[0]))
    zero_acc = tuple((jnp.zeros_like(replica_place) for replica_place in block_weight_bundle))
    totals, (outputs, input_grads) = lax.scan(one_sequence, zero_acc, (block_entry_tokens, result_cotangent))
    return (outputs, input_grads) + totals
```

```python
import functools

import jax
import jax.numpy as jnp
from jax import lax
from jax.experimental import pallas as pl
from jax.experimental.pallas import tpu as pltpu
from jax.sharding import PartitionSpec as P

HD = 64
LANES = 128
EPS = 1e-05
NEG = -1e30
FACTOR = HD ** (-0.5)
VMEM_BYTES = 40 * 1024 * 1024


def standardize_features(values, gain, shift):
    center = values - jnp.mean(values, -1, keepdims=True)
    spread = jnp.mean(center * center, -1, keepdims=True)
    return center * lax.rsqrt(spread + EPS) * gain + shift


def gelu_apply(values):
    return jax.nn.gelu(values, approximate=True)


def dot_nt(left, right):
    return lax.dot_general(
        left, right, (((1,), (1,)), ((), ())), preferred_element_type=jnp.float32
    )


def dot_tn(left, right):
    return lax.dot_general(
        left, right, (((0,), (0,)), ((), ())), preferred_element_type=jnp.float32
    )


def dot_nn(left, right):
    return jnp.dot(left, right, preferred_element_type=jnp.float32)


def head_mask(head, dtype):
    lane = lax.broadcasted_iota(jnp.int32, (1, LANES), 1)
    return (lane // HD == head).astype(dtype)


def row_step(rows):
    return min(256, rows)


def causal(scores, start):
    query_pos = start + lax.broadcasted_iota(jnp.int32, scores.shape, 0)
    key_pos = lax.broadcasted_iota(jnp.int32, scores.shape, 1)
    return jnp.where(key_pos <= query_pos, scores, NEG)


def before(scores, limit):
    key_pos = lax.broadcasted_iota(jnp.int32, scores.shape, 1)
    return jnp.where(key_pos < limit, scores, NEG)


def forward_kernel(limit_ref, q_ref, k_ref, v_ref, kr_ref, vr_ref, ctx_ref, lse_ref):
    rows = q_ref.shape[0]
    step = row_step(rows)
    limit = limit_ref[0]
    lane = lax.broadcasted_iota(jnp.int32, (step, LANES), 1)
    for start in range(0, rows, step):
        end = start + step
        context = jnp.zeros((step, LANES), jnp.float32)
        sums = []
        for head in range(2):
            mask = head_mask(head, jnp.bfloat16)
            queries = q_ref[start:end] * mask
            own = causal(dot_nt(queries, k_ref[:end]) * FACTOR, start)
            far = before(dot_nt(queries, kr_ref[...]) * FACTOR, limit)
            highest = jnp.maximum(
                jnp.max(own, -1, keepdims=True), jnp.max(far, -1, keepdims=True)
            )
            own = jnp.exp(own - highest)
            far = jnp.exp(far - highest)
            total = jnp.sum(own, -1, keepdims=True) + jnp.sum(far, -1, keepdims=True)
            inverse = 1.0 / total
            context = context + dot_nn((own * inverse).astype(jnp.bfloat16), v_ref[:end] * mask)
            context = context + dot_nn((far * inverse).astype(jnp.bfloat16), vr_ref[...] * mask)
            sums.append(highest + jnp.log(total))
        ctx_ref[start:end] = context.astype(jnp.bfloat16)
        lse_ref[start:end] = jnp.where(lane < HD, sums[0], sums[1])


def back_block(q_ref, g_ref, ctx_ref, lse_ref, keys, values, start, end, head, cut):
    mask = head_mask(head, jnp.bfloat16)
    queries = q_ref[start:end] * mask
    grads = g_ref[start:end] * mask
    inner = jnp.sum(
        grads.astype(jnp.float32) * ctx_ref[start:end].astype(jnp.float32), -1, keepdims=True
    )
    logsum = lse_ref[start:end, head * HD : head * HD + 1]
    probab = jnp.exp(cut(dot_nt(queries, keys) * FACTOR) - logsum)
    delta = (probab * (dot_nt(grads, values) - inner)).astype(jnp.bfloat16)
    return (
        dot_nn(delta, keys * mask) * FACTOR,
        dot_tn(delta, queries) * FACTOR,
        dot_tn(probab.astype(jnp.bfloat16), grads),
    )


def back_far_kernel(
    limit_ref, q_ref, g_ref, ctx_ref, lse_ref, kr_ref, vr_ref, dq_ref, dk_ref, dv_ref
):
    rows = q_ref.shape[0]
    step = row_step(rows)
    limit = limit_ref[0]
    dk = jnp.zeros(kr_ref.shape, jnp.float32)
    dv = jnp.zeros(kr_ref.shape, jnp.float32)
    for start in range(0, rows, step):
        end = start + step
        dq = jnp.zeros((step, LANES), jnp.float32)
        for head in range(2):
            one, two, three = back_block(
                q_ref, g_ref, ctx_ref, lse_ref, kr_ref[...], vr_ref[...], start, end, head,
                lambda s: before(s, limit),
            )
            dq, dk, dv = dq + one, dk + two, dv + three
        dq_ref[start:end] = dq
    dk_ref[...] = dk.astype(jnp.bfloat16)
    dv_ref[...] = dv.astype(jnp.bfloat16)


def back_own_kernel(
    q_ref, g_ref, ctx_ref, lse_ref, k_ref, v_ref, dqfar_ref, dq_ref, dk_ref, dv_ref
):
    rows = q_ref.shape[0]
    step = row_step(rows)
    dk_ref[...] = jnp.zeros(dk_ref.shape, jnp.float32)
    dv_ref[...] = jnp.zeros(dv_ref.shape, jnp.float32)
    for start in range(0, rows, step):
        end = start + step
        dq = dqfar_ref[start:end]
        for head in range(2):
            one, two, three = back_block(
                q_ref, g_ref, ctx_ref, lse_ref, k_ref[:end], v_ref[:end], start, end, head,
                lambda s: causal(s, start),
            )
            dq = dq + one
            dk_ref[:end] += two
            dv_ref[:end] += three
        dq_ref[start:end] = dq.astype(jnp.bfloat16)


def pair_spec(rows, base):
    return pl.BlockSpec((rows, LANES), lambda pair: (0, base + pair))


def cost(rows, keys, width, products):
    return pl.CostEstimate(
        flops=4 * 2 * products * rows * keys * width,
        bytes_accessed=2 * width * (4 * rows + 4 * keys),
        transcendentals=rows * keys * width // HD,
    )


LIMIT_SPEC = pl.BlockSpec(memory_space=pltpu.SMEM)
PARAMS = pltpu.CompilerParams(vmem_limit_bytes=VMEM_BYTES)


def attend(limit, queries, keyvals, far):
    rows, width = queries.shape
    extent = far.shape[0]
    pairs = width // LANES
    return pl.pallas_call(
        forward_kernel,
        grid=(pairs,),
        in_specs=[
            LIMIT_SPEC,
            pair_spec(rows, 0),
            pair_spec(rows, 0),
            pair_spec(rows, pairs),
            pair_spec(extent, 0),
            pair_spec(extent, pairs),
        ],
        out_specs=[pair_spec(rows, 0), pair_spec(rows, 0)],
        out_shape=[
            jax.ShapeDtypeStruct((rows, width), jnp.bfloat16),
            jax.ShapeDtypeStruct((rows, width), jnp.float32),
        ],
        compiler_params=PARAMS,
        cost_estimate=cost(rows, rows + extent, width, 2),
        name="attend",
    )(limit, queries, keyvals, keyvals, far, far)


def attend_back_far(limit, queries, grads, context, logsum, far):
    rows, width = queries.shape
    extent = far.shape[0]
    pairs = width // LANES
    return pl.pallas_call(
        back_far_kernel,
        grid=(pairs,),
        in_specs=[LIMIT_SPEC]
        + [pair_spec(rows, 0)] * 4
        + [pair_spec(extent, 0), pair_spec(extent, pairs)],
        out_specs=[pair_spec(rows, 0), pair_spec(extent, 0), pair_spec(extent, 0)],
        out_shape=[
            jax.ShapeDtypeStruct((rows, width), jnp.float32),
            jax.ShapeDtypeStruct((extent, width), jnp.bfloat16),
            jax.ShapeDtypeStruct((extent, width), jnp.bfloat16),
        ],
        compiler_params=PARAMS,
        cost_estimate=cost(rows, extent, width, 5),
        name="attend_back_far",
    )(limit, queries, grads, context, logsum, far, far)


def attend_back_own(queries, grads, context, logsum, keyvals, dq_far):
    rows, width = queries.shape
    pairs = width // LANES
    return pl.pallas_call(
        back_own_kernel,
        grid=(pairs,),
        in_specs=[pair_spec(rows, 0)] * 4
        + [pair_spec(rows, 0), pair_spec(rows, pairs), pair_spec(rows, 0)],
        out_specs=[pair_spec(rows, 0)] * 3,
        out_shape=[
            jax.ShapeDtypeStruct((rows, width), jnp.bfloat16),
            jax.ShapeDtypeStruct((rows, width), jnp.float32),
            jax.ShapeDtypeStruct((rows, width), jnp.float32),
        ],
        compiler_params=PARAMS,
        cost_estimate=cost(rows, rows, width, 5),
        name="attend_back_own",
    )(queries, grads, context, logsum, keyvals, keyvals, dq_far)


def pack_rows(pieces, rows):
    joined = jnp.concatenate(pieces, -1)
    spare = rows * LANES - joined.shape[-1]
    padded = jnp.pad(joined, ((0, 0), (0, spare)))
    return padded.reshape(joined.shape[0] * rows, LANES)


def unpack_rows(packed, shards, lengths):
    flat = packed.reshape(shards, -1)
    pieces, at = [], 0
    for length in lengths:
        pieces.append(flat[:, at : at + length].reshape(-1))
        at += length
    return pieces


def swap_sum(value, ranks):
    if ranks == 2:
        other = lax.ppermute(value, "seq", [(0, 1), (1, 0)])
        return value.astype(jnp.float32) + other.astype(jnp.float32)
    return lax.psum(value, "seq").astype(jnp.float32)


def local(
    block_entry_tokens,
    result_cotangent,
    leading_scale_factor,
    leading_bias_vector,
    query_key_value_matrix,
    query_key_value_bias,
    attention_exit_matrix,
    attention_exit_bias,
    latter_scale_factor,
    latter_bias_vector,
    expand_projection_matrix,
    expand_projection_offset,
    contract_projection_matrix,
    contract_projection_offset,
    shards,
    ranks,
):
    f32, bf16 = jnp.float32, jnp.bfloat16
    hidden = block_entry_tokens.reshape(-1, block_entry_tokens.shape[-1]).astype(f32)
    tokens, width = hidden.shape
    place = lax.axis_index("seq")
    limit = (place * tokens).astype(jnp.int32).reshape(1)
    vectors = (
        leading_scale_factor,
        leading_bias_vector,
        query_key_value_bias,
        attention_exit_bias,
        latter_scale_factor,
        latter_bias_vector,
        expand_projection_offset,
        contract_projection_offset,
    )
    lengths = [vector.shape[0] for vector in vectors]
    rows = query_key_value_matrix.shape[0]
    small = pack_rows([vector[None] for vector in vectors], rows)
    attn_whole = lax.all_gather(
        jnp.concatenate([query_key_value_matrix, attention_exit_matrix, small], 1),
        "dp",
        axis=0,
        tiled=True,
    )
    w_up = lax.all_gather(expand_projection_matrix, "dp", axis=0, tiled=True)
    w_down = lax.all_gather(contract_projection_matrix, "dp", axis=0, tiled=True)
    w_q = attn_whole[:, :width]
    w_kv = attn_whole[:, width : 3 * width]
    w_qkv = attn_whole[:, : 3 * width]
    w_out = attn_whole[:, 3 * width : 4 * width]
    gain_one, shift_one, b_qkv, b_out, gain_two, shift_two, b_up, b_down = (
        vector.astype(f32) for vector in unpack_rows(attn_whole[:, 4 * width :], shards, lengths)
    )

    normed_one, pull_one = jax.vjp(standardize_features, hidden, gain_one, shift_one)
    h_one = normed_one.astype(bf16)
    keyvals = (dot_nn(h_one, w_kv) + b_qkv[width:]).astype(bf16)
    if ranks == 2:
        far = lax.ppermute(keyvals, "seq", [(0, 1)])
    else:
        far = lax.all_gather(keyvals, "seq", axis=0, tiled=True)
    queries = (dot_nn(h_one, w_q) + b_qkv[:width]).astype(bf16)
    context, logsum = attend(limit, queries, keyvals, far)
    resid = hidden + dot_nn(context, w_out) + b_out

    normed_two, pull_two = jax.vjp(standardize_features, resid, gain_two, shift_two)
    h_two = normed_two.astype(bf16)
    upact = dot_nn(h_two, w_up) + b_up
    activ, gelu_pull = jax.vjp(gelu_apply, upact)
    act_low = activ.astype(bf16)
    out_delta = result_cotangent.reshape(tokens, width)
    down_part = dot_tn(act_low, out_delta).astype(bf16)
    down_part, act_low, out_delta = lax.optimization_barrier((down_part, act_low, out_delta))
    down_owned = lax.psum_scatter(down_part, "dp", scatter_dimension=0, tiled=True)
    out_float = out_delta.astype(f32)
    downshift_grad = jnp.sum(out_float, 0)
    up_delta = gelu_pull(dot_nt(out_delta, w_down))[0].astype(bf16)
    upshift_grad = jnp.sum(up_delta.astype(f32), 0)
    up_part = dot_tn(h_two, up_delta).astype(bf16)
    up_part, up_delta = lax.optimization_barrier((up_part, up_delta))
    up_owned = lax.psum_scatter(up_part, "dp", scatter_dimension=0, tiled=True)
    output = resid + dot_nn(act_low, w_down) + b_down
    norm_two_delta = dot_nt(up_delta, w_up)
    resid_part, midgain_grad, midshift_grad = pull_two(norm_two_delta)
    resid_grad = out_float + resid_part
    proj_delta = resid_grad.astype(bf16)
    outshift_grad = jnp.sum(proj_delta.astype(f32), 0)
    ctx_delta = dot_nt(proj_delta, w_out).astype(bf16)
    dq_far, dk_far, dv_far = attend_back_far(limit, queries, ctx_delta, context, logsum, far)
    if ranks == 2:
        dk_back = lax.ppermute(dk_far, "seq", [(1, 0)])
        dv_back = lax.ppermute(dv_far, "seq", [(1, 0)])
    else:
        dk_back = lax.psum_scatter(dk_far, "seq", scatter_dimension=0, tiled=True)
        dv_back = lax.psum_scatter(dv_far, "seq", scatter_dimension=0, tiled=True)
    dq, dk_own, dv_own = attend_back_own(queries, ctx_delta, context, logsum, keyvals, dq_far)
    out_part = dot_tn(context, proj_delta).astype(bf16)
    qkv_delta = jnp.concatenate(
        [
            dq,
            (dk_own + dk_back.astype(f32)).astype(bf16),
            (dv_own + dv_back.astype(f32)).astype(bf16),
        ],
        1,
    )
    qkvshift_grad = jnp.sum(qkv_delta.astype(f32), 0)
    qkv_part = dot_tn(h_one, qkv_delta).astype(bf16)
    input_portion, prenorm_gain_gradient, prenorm_shift_gradient = pull_one(
        dot_nt(qkv_delta, w_qkv)
    )
    input_grad = resid_grad + input_portion
    small_parts = (
        prenorm_gain_gradient,
        prenorm_shift_gradient,
        qkvshift_grad,
        outshift_grad,
        midgain_grad,
        midshift_grad,
        upshift_grad,
        downshift_grad,
    )
    small_part = pack_rows(
        [part.astype(bf16).reshape(shards, -1) for part in small_parts], rows
    )
    attn_owned = lax.psum_scatter(
        jnp.concatenate([qkv_part, out_part, small_part], 1),
        "dp",
        scatter_dimension=0,
        tiled=True,
    )
    upmatrix_grad = swap_sum(up_owned, ranks)
    downmatrix_grad = swap_sum(down_owned, ranks)
    attn_sum = swap_sum(attn_owned, ranks)
    gain_g, shift_g, qkvshift, outshift, midgain, midshift, upshift, downshift = unpack_rows(
        attn_sum[:, 4 * width :], 1, lengths
    )
    return (
        output.reshape(1, tokens, width),
        input_grad.reshape(1, tokens, width),
        gain_g,
        shift_g,
        attn_sum[:, : 3 * width],
        qkvshift,
        attn_sum[:, 3 * width : 4 * width],
        outshift,
        midgain,
        midshift,
        upmatrix_grad,
        upshift,
        downmatrix_grad,
        downshift,
    )


def solution(mesh):
    in_specs = (
        P("dp", "seq", None),
        P("dp", "seq", None),
        P("dp"),
        P("dp"),
        P("dp", None),
        P("dp"),
        P("dp", None),
        P("dp"),
        P("dp"),
        P("dp"),
        P("dp", None),
        P("dp"),
        P("dp", None),
        P("dp"),
    )
    out_specs = (
        P("dp", "seq", None),
        P("dp", "seq", None),
        P("dp"),
        P("dp"),
        P("dp", None),
        P("dp"),
        P("dp", None),
        P("dp"),
        P("dp"),
        P("dp"),
        P("dp", None),
        P("dp"),
        P("dp", None),
        P("dp"),
    )
    body = functools.partial(local, shards=mesh.shape["dp"], ranks=mesh.shape["seq"])
    return jax.shard_map(body, mesh=mesh, in_specs=in_specs, out_specs=out_specs, check_vma=False)
```

```python
import functools

import jax
import jax.numpy as jnp
from jax import lax
from jax.experimental import pallas as pl
from jax.experimental.pallas import tpu as pltpu
from jax.sharding import PartitionSpec as P

HD = 64
LANES = 128
EPS = 1e-05
NEG = -1e30
FACTOR = HD ** (-0.5)
VMEM_BYTES = 40 * 1024 * 1024


def standardize_features(values, gain, shift):
    center = values - jnp.mean(values, -1, keepdims=True)
    spread = jnp.mean(center * center, -1, keepdims=True)
    return center * lax.rsqrt(spread + EPS) * gain + shift


def gelu_apply(values):
    return jax.nn.gelu(values, approximate=True)


def dot_nt(left, right):
    return lax.dot_general(
        left, right, (((1,), (1,)), ((), ())), preferred_element_type=jnp.float32
    )


def dot_tn(left, right):
    return lax.dot_general(
        left, right, (((0,), (0,)), ((), ())), preferred_element_type=jnp.float32
    )


def dot_nn(left, right):
    return jnp.dot(left, right, preferred_element_type=jnp.float32)


def head_mask(head, dtype):
    lane = lax.broadcasted_iota(jnp.int32, (1, LANES), 1)
    return (lane // HD == head).astype(dtype)


def row_step(rows):
    return min(256, rows)


def causal(scores, start):
    query_pos = start + lax.broadcasted_iota(jnp.int32, scores.shape, 0)
    key_pos = lax.broadcasted_iota(jnp.int32, scores.shape, 1)
    return jnp.where(key_pos <= query_pos, scores, NEG)


def before(scores, limit):
    key_pos = lax.broadcasted_iota(jnp.int32, scores.shape, 1)
    return jnp.where(key_pos < limit, scores, NEG)


def forward_kernel(limit_ref, q_ref, k_ref, v_ref, kr_ref, vr_ref, ctx_ref, lse_ref):
    rows = q_ref.shape[0]
    step = row_step(rows)
    limit = limit_ref[0]
    lane = lax.broadcasted_iota(jnp.int32, (step, LANES), 1)
    for start in range(0, rows, step):
        end = start + step
        context = jnp.zeros((step, LANES), jnp.float32)
        sums = []
        for head in range(2):
            mask = head_mask(head, jnp.bfloat16)
            queries = q_ref[start:end] * mask
            own = causal(dot_nt(queries, k_ref[:end]) * FACTOR, start)
            far = before(dot_nt(queries, kr_ref[...]) * FACTOR, limit)
            highest = jnp.maximum(
                jnp.max(own, -1, keepdims=True), jnp.max(far, -1, keepdims=True)
            )
            own = jnp.exp(own - highest)
            far = jnp.exp(far - highest)
            total = jnp.sum(own, -1, keepdims=True) + jnp.sum(far, -1, keepdims=True)
            inverse = 1.0 / total
            context = context + dot_nn((own * inverse).astype(jnp.bfloat16), v_ref[:end] * mask)
            context = context + dot_nn((far * inverse).astype(jnp.bfloat16), vr_ref[...] * mask)
            sums.append(highest + jnp.log(total))
        ctx_ref[start:end] = context.astype(jnp.bfloat16)
        lse_ref[start:end] = jnp.where(lane < HD, sums[0], sums[1])


def back_block(q_ref, g_ref, ctx_ref, lse_ref, keys, values, start, end, head, cut):
    mask = head_mask(head, jnp.bfloat16)
    queries = q_ref[start:end] * mask
    grads = g_ref[start:end] * mask
    inner = jnp.sum(
        grads.astype(jnp.float32) * ctx_ref[start:end].astype(jnp.float32), -1, keepdims=True
    )
    logsum = lse_ref[start:end, head * HD : head * HD + 1]
    probab = jnp.exp(cut(dot_nt(queries, keys) * FACTOR) - logsum)
    delta = (probab * (dot_nt(grads, values) - inner)).astype(jnp.bfloat16)
    return (
        dot_nn(delta, keys * mask) * FACTOR,
        dot_tn(delta, queries) * FACTOR,
        dot_tn(probab.astype(jnp.bfloat16), grads),
    )


def back_far_kernel(
    limit_ref, q_ref, g_ref, ctx_ref, lse_ref, kr_ref, vr_ref, dq_ref, dk_ref, dv_ref
):
    rows = q_ref.shape[0]
    step = row_step(rows)
    limit = limit_ref[0]
    dk = jnp.zeros(kr_ref.shape, jnp.float32)
    dv = jnp.zeros(kr_ref.shape, jnp.float32)
    for start in range(0, rows, step):
        end = start + step
        dq = jnp.zeros((step, LANES), jnp.float32)
        for head in range(2):
            one, two, three = back_block(
                q_ref, g_ref, ctx_ref, lse_ref, kr_ref[...], vr_ref[...], start, end, head,
                lambda s: before(s, limit),
            )
            dq, dk, dv = dq + one, dk + two, dv + three
        dq_ref[start:end] = dq
    dk_ref[...] = dk.astype(jnp.bfloat16)
    dv_ref[...] = dv.astype(jnp.bfloat16)


def back_own_kernel(
    q_ref, g_ref, ctx_ref, lse_ref, k_ref, v_ref, dqfar_ref, dq_ref, dk_ref, dv_ref
):
    rows = q_ref.shape[0]
    step = row_step(rows)
    dk_ref[...] = jnp.zeros(dk_ref.shape, jnp.float32)
    dv_ref[...] = jnp.zeros(dv_ref.shape, jnp.float32)
    for start in range(0, rows, step):
        end = start + step
        dq = dqfar_ref[start:end]
        for head in range(2):
            one, two, three = back_block(
                q_ref, g_ref, ctx_ref, lse_ref, k_ref[:end], v_ref[:end], start, end, head,
                lambda s: causal(s, start),
            )
            dq = dq + one
            dk_ref[:end] += two
            dv_ref[:end] += three
        dq_ref[start:end] = dq.astype(jnp.bfloat16)


def pair_spec(rows, base):
    return pl.BlockSpec((rows, LANES), lambda pair: (0, base + pair))


def cost(rows, keys, width, products):
    return pl.CostEstimate(
        flops=4 * 2 * products * rows * keys * width,
        bytes_accessed=2 * width * (4 * rows + 4 * keys),
        transcendentals=rows * keys * width // HD,
    )


LIMIT_SPEC = pl.BlockSpec(memory_space=pltpu.SMEM)
PARAMS = pltpu.CompilerParams(vmem_limit_bytes=VMEM_BYTES)


def attend(limit, queries, keyvals, far):
    rows, width = queries.shape
    extent = far.shape[0]
    pairs = width // LANES
    return pl.pallas_call(
        forward_kernel,
        grid=(pairs,),
        in_specs=[
            LIMIT_SPEC,
            pair_spec(rows, 0),
            pair_spec(rows, 0),
            pair_spec(rows, pairs),
            pair_spec(extent, 0),
            pair_spec(extent, pairs),
        ],
        out_specs=[pair_spec(rows, 0), pair_spec(rows, 0)],
        out_shape=[
            jax.ShapeDtypeStruct((rows, width), jnp.bfloat16),
            jax.ShapeDtypeStruct((rows, width), jnp.float32),
        ],
        compiler_params=PARAMS,
        cost_estimate=cost(rows, rows + extent, width, 2),
        name="attend",
    )(limit, queries, keyvals, keyvals, far, far)


def attend_back_far(limit, queries, grads, context, logsum, far):
    rows, width = queries.shape
    extent = far.shape[0]
    pairs = width // LANES
    return pl.pallas_call(
        back_far_kernel,
        grid=(pairs,),
        in_specs=[LIMIT_SPEC]
        + [pair_spec(rows, 0)] * 4
        + [pair_spec(extent, 0), pair_spec(extent, pairs)],
        out_specs=[pair_spec(rows, 0), pair_spec(extent, 0), pair_spec(extent, 0)],
        out_shape=[
            jax.ShapeDtypeStruct((rows, width), jnp.float32),
            jax.ShapeDtypeStruct((extent, width), jnp.bfloat16),
            jax.ShapeDtypeStruct((extent, width), jnp.bfloat16),
        ],
        compiler_params=PARAMS,
        cost_estimate=cost(rows, extent, width, 5),
        name="attend_back_far",
    )(limit, queries, grads, context, logsum, far, far)


def attend_back_own(queries, grads, context, logsum, keyvals, dq_far):
    rows, width = queries.shape
    pairs = width // LANES
    return pl.pallas_call(
        back_own_kernel,
        grid=(pairs,),
        in_specs=[pair_spec(rows, 0)] * 4
        + [pair_spec(rows, 0), pair_spec(rows, pairs), pair_spec(rows, 0)],
        out_specs=[pair_spec(rows, 0)] * 3,
        out_shape=[
            jax.ShapeDtypeStruct((rows, width), jnp.bfloat16),
            jax.ShapeDtypeStruct((rows, width), jnp.float32),
            jax.ShapeDtypeStruct((rows, width), jnp.float32),
        ],
        compiler_params=PARAMS,
        cost_estimate=cost(rows, rows, width, 5),
        name="attend_back_own",
    )(queries, grads, context, logsum, keyvals, keyvals, dq_far)


def pack_rows(pieces, rows):
    joined = jnp.concatenate(pieces, -1)
    spare = rows * LANES - joined.shape[-1]
    padded = jnp.pad(joined, ((0, 0), (0, spare)))
    return padded.reshape(joined.shape[0] * rows, LANES)


def unpack_rows(packed, shards, lengths):
    flat = packed.reshape(shards, -1)
    pieces, at = [], 0
    for length in lengths:
        pieces.append(flat[:, at : at + length].reshape(-1))
        at += length
    return pieces


def pick(blocks, index):
    return lax.dynamic_index_in_dim(blocks, index, 1, keepdims=False)


def swap_half(blocks, axis, pairs, mine):
    other = lax.ppermute(pick(blocks, 1 - mine), axis, pairs)
    total = pick(blocks, mine).astype(jnp.float32) + other.astype(jnp.float32)
    return total.astype(jnp.bfloat16)


def sum_cores(part, shards):
    blocks = part.reshape(shards // 2, 2, part.shape[0] // shards, part.shape[-1])
    core = lax.rem(lax.axis_index("dp"), 2)
    pairs = [(i, i + 1 - 2 * (i % 2)) for i in range(shards)]
    return swap_half(blocks, "dp", pairs, core)


def sum_ranks(held, ranks):
    if ranks != 2:
        return held
    blocks = held.reshape(held.shape[0], 2, held.shape[1] // 2, held.shape[2])
    return swap_half(blocks, "seq", [(0, 1), (1, 0)], lax.axis_index("seq"))


def sum_chips(held, shards):
    return lax.psum_scatter(
        held.reshape(-1, held.shape[-1]),
        "dp",
        scatter_dimension=0,
        axis_index_groups=[list(range(0, shards, 2)), list(range(1, shards, 2))],
        tiled=True,
    )


def finish_sum(owned, ranks, seq_first):
    if ranks != 2:
        return lax.psum(owned, "seq").astype(jnp.float32)
    other = lax.ppermute(owned, "seq", [(0, 1), (1, 0)])
    if not seq_first:
        return owned.astype(jnp.float32) + other.astype(jnp.float32)
    first = lax.axis_index("seq") == 0
    top = jnp.where(first, owned, other)
    bottom = jnp.where(first, other, owned)
    return jnp.concatenate([top, bottom], 0).astype(jnp.float32)


def local(
    block_entry_tokens,
    result_cotangent,
    leading_scale_factor,
    leading_bias_vector,
    query_key_value_matrix,
    query_key_value_bias,
    attention_exit_matrix,
    attention_exit_bias,
    latter_scale_factor,
    latter_bias_vector,
    expand_projection_matrix,
    expand_projection_offset,
    contract_projection_matrix,
    contract_projection_offset,
    shards,
    ranks,
):
    f32, bf16 = jnp.float32, jnp.bfloat16
    hidden = block_entry_tokens.reshape(-1, block_entry_tokens.shape[-1]).astype(f32)
    tokens, width = hidden.shape
    place = lax.axis_index("seq")
    limit = (place * tokens).astype(jnp.int32).reshape(1)
    vectors = (
        leading_scale_factor,
        leading_bias_vector,
        query_key_value_bias,
        attention_exit_bias,
        latter_scale_factor,
        latter_bias_vector,
        expand_projection_offset,
        contract_projection_offset,
    )
    lengths = [vector.shape[0] for vector in vectors]
    rows = query_key_value_matrix.shape[0]
    small = pack_rows([vector[None] for vector in vectors], rows)
    attn_whole = lax.all_gather(
        jnp.concatenate([query_key_value_matrix, attention_exit_matrix, small], 1),
        "dp",
        axis=0,
        tiled=True,
    )
    w_up = lax.all_gather(expand_projection_matrix, "dp", axis=0, tiled=True)
    w_down = lax.all_gather(contract_projection_matrix, "dp", axis=0, tiled=True)
    w_q = attn_whole[:, :width]
    w_kv = attn_whole[:, width : 3 * width]
    w_qkv = attn_whole[:, : 3 * width]
    w_out = attn_whole[:, 3 * width : 4 * width]
    gain_one, shift_one, b_qkv, b_out, gain_two, shift_two, b_up, b_down = (
        vector.astype(f32) for vector in unpack_rows(attn_whole[:, 4 * width :], shards, lengths)
    )

    normed_one, pull_one = jax.vjp(standardize_features, hidden, gain_one, shift_one)
    h_one = normed_one.astype(bf16)
    keyvals = (dot_nn(h_one, w_kv) + b_qkv[width:]).astype(bf16)
    if ranks == 2:
        far = lax.ppermute(keyvals, "seq", [(0, 1)])
    else:
        far = lax.all_gather(keyvals, "seq", axis=0, tiled=True)
    queries = (dot_nn(h_one, w_q) + b_qkv[:width]).astype(bf16)
    context, logsum = attend(limit, queries, keyvals, far)
    resid = hidden + dot_nn(context, w_out) + b_out

    normed_two, pull_two = jax.vjp(standardize_features, resid, gain_two, shift_two)
    h_two = normed_two.astype(bf16)
    upact = dot_nn(h_two, w_up) + b_up
    activ, gelu_pull = jax.vjp(gelu_apply, upact)
    act_low = activ.astype(bf16)
    out_delta = result_cotangent.reshape(tokens, width)
    down_part = dot_tn(act_low, out_delta).astype(bf16)
    down_held = sum_cores(down_part, shards)
    down_held, act_low, out_delta = lax.optimization_barrier((down_held, act_low, out_delta))
    down_held = sum_ranks(down_held, ranks)
    out_float = out_delta.astype(f32)
    downshift_grad = jnp.sum(out_float, 0)
    up_delta = gelu_pull(dot_nt(out_delta, w_down))[0].astype(bf16)
    upshift_grad = jnp.sum(up_delta.astype(f32), 0)
    up_part = dot_tn(h_two, up_delta).astype(bf16)
    up_part, up_delta, down_held = lax.optimization_barrier((up_part, up_delta, down_held))
    down_owned = sum_chips(down_held, shards)
    up_held = sum_cores(up_part, shards)
    output = resid + dot_nn(act_low, w_down) + b_down
    norm_two_delta = dot_nt(up_delta, w_up)
    resid_part, midgain_grad, midshift_grad = pull_two(norm_two_delta)
    resid_grad = out_float + resid_part
    proj_delta = resid_grad.astype(bf16)
    outshift_grad = jnp.sum(proj_delta.astype(f32), 0)
    ctx_delta = dot_nt(proj_delta, w_out).astype(bf16)
    dq_far, dk_far, dv_far = attend_back_far(limit, queries, ctx_delta, context, logsum, far)
    if ranks == 2:
        dk_back = lax.ppermute(dk_far, "seq", [(1, 0)])
        dv_back = lax.ppermute(dv_far, "seq", [(1, 0)])
    else:
        dk_back = lax.psum_scatter(dk_far, "seq", scatter_dimension=0, tiled=True)
        dv_back = lax.psum_scatter(dv_far, "seq", scatter_dimension=0, tiled=True)
    up_held, dq_far = lax.optimization_barrier((up_held, dq_far))
    up_owned = sum_chips(up_held, shards)
    dq, dk_own, dv_own = attend_back_own(queries, ctx_delta, context, logsum, keyvals, dq_far)
    out_part = dot_tn(context, proj_delta).astype(bf16)
    down_owned, dq, dk_own, dv_own = lax.optimization_barrier((down_owned, dq, dk_own, dv_own))
    qkv_delta = jnp.concatenate(
        [
            dq,
            (dk_own + dk_back.astype(f32)).astype(bf16),
            (dv_own + dv_back.astype(f32)).astype(bf16),
        ],
        1,
    )
    qkvshift_grad = jnp.sum(qkv_delta.astype(f32), 0)
    qkv_part = dot_tn(h_one, qkv_delta).astype(bf16)
    input_portion, prenorm_gain_gradient, prenorm_shift_gradient = pull_one(
        dot_nt(qkv_delta, w_qkv)
    )
    input_grad = resid_grad + input_portion
    small_parts = (
        prenorm_gain_gradient,
        prenorm_shift_gradient,
        qkvshift_grad,
        outshift_grad,
        midgain_grad,
        midshift_grad,
        upshift_grad,
        downshift_grad,
    )
    small_part = pack_rows(
        [part.astype(bf16).reshape(shards, -1) for part in small_parts], rows
    )
    attn_held = sum_ranks(
        sum_cores(jnp.concatenate([qkv_part, out_part, small_part], 1), shards), ranks
    )
    up_owned, attn_held = lax.optimization_barrier((up_owned, attn_held))
    attn_owned = sum_chips(attn_held, shards)
    upmatrix_grad = finish_sum(up_owned, ranks, False)
    downmatrix_grad = finish_sum(down_owned, ranks, True)
    attn_sum = finish_sum(attn_owned, ranks, True)
    gain_g, shift_g, qkvshift, outshift, midgain, midshift, upshift, downshift = unpack_rows(
        attn_sum[:, 4 * width :], 1, lengths
    )
    return (
        output.reshape(1, tokens, width),
        input_grad.reshape(1, tokens, width),
        gain_g,
        shift_g,
        attn_sum[:, : 3 * width],
        qkvshift,
        attn_sum[:, 3 * width : 4 * width],
        outshift,
        midgain,
        midshift,
        upmatrix_grad,
        upshift,
        downmatrix_grad,
        downshift,
    )


def solution(mesh):
    in_specs = (
        P("dp", "seq", None),
        P("dp", "seq", None),
        P("dp"),
        P("dp"),
        P("dp", None),
        P("dp"),
        P("dp", None),
        P("dp"),
        P("dp"),
        P("dp"),
        P("dp", None),
        P("dp"),
        P("dp", None),
        P("dp"),
    )
    out_specs = (
        P("dp", "seq", None),
        P("dp", "seq", None),
        P("dp"),
        P("dp"),
        P("dp", None),
        P("dp"),
        P("dp", None),
        P("dp"),
        P("dp"),
        P("dp"),
        P("dp", None),
        P("dp"),
        P("dp", None),
        P("dp"),
    )
    body = functools.partial(local, shards=mesh.shape["dp"], ranks=mesh.shape["seq"])
    return jax.shard_map(body, mesh=mesh, in_specs=in_specs, out_specs=out_specs, check_vma=False)
```

```python
import functools

import jax
import jax.numpy as jnp
from jax import lax
from jax.experimental import pallas as pl
from jax.experimental.pallas import tpu as pltpu
from jax.sharding import PartitionSpec as P

HD = 64
LANES = 128
EPS = 1e-05
NEG = -1e30
FACTOR = HD ** (-0.5)
VMEM_BYTES = 40 * 1024 * 1024


def standardize_features(values, gain, shift):
    center = values - jnp.mean(values, -1, keepdims=True)
    spread = jnp.mean(center * center, -1, keepdims=True)
    return center * lax.rsqrt(spread + EPS) * gain + shift


def gelu_apply(values):
    return jax.nn.gelu(values, approximate=True)


def dot_nt(left, right):
    return lax.dot_general(
        left, right, (((1,), (1,)), ((), ())), preferred_element_type=jnp.float32
    )


def dot_tn(left, right):
    return lax.dot_general(
        left, right, (((0,), (0,)), ((), ())), preferred_element_type=jnp.float32
    )


def dot_nn(left, right):
    return jnp.dot(left, right, preferred_element_type=jnp.float32)


def head_mask(head, dtype):
    lane = lax.broadcasted_iota(jnp.int32, (1, LANES), 1)
    return (lane // HD == head).astype(dtype)


def row_step(rows):
    return min(256, rows)


def causal(scores, start):
    query_pos = start + lax.broadcasted_iota(jnp.int32, scores.shape, 0)
    key_pos = lax.broadcasted_iota(jnp.int32, scores.shape, 1)
    return jnp.where(key_pos <= query_pos, scores, NEG)


def before(scores, limit):
    key_pos = lax.broadcasted_iota(jnp.int32, scores.shape, 1)
    return jnp.where(key_pos < limit, scores, NEG)


def forward_kernel(limit_ref, q_ref, k_ref, v_ref, kr_ref, vr_ref, ctx_ref, lse_ref):
    rows = q_ref.shape[0]
    step = row_step(rows)
    limit = limit_ref[0]
    lane = lax.broadcasted_iota(jnp.int32, (step, LANES), 1)
    for start in range(0, rows, step):
        end = start + step
        context = jnp.zeros((step, LANES), jnp.float32)
        sums = []
        for head in range(2):
            mask = head_mask(head, jnp.bfloat16)
            queries = q_ref[start:end] * mask
            own = causal(dot_nt(queries, k_ref[:end]) * FACTOR, start)
            far = before(dot_nt(queries, kr_ref[...]) * FACTOR, limit)
            highest = jnp.maximum(
                jnp.max(own, -1, keepdims=True), jnp.max(far, -1, keepdims=True)
            )
            own = jnp.exp(own - highest)
            far = jnp.exp(far - highest)
            total = jnp.sum(own, -1, keepdims=True) + jnp.sum(far, -1, keepdims=True)
            inverse = 1.0 / total
            context = context + dot_nn((own * inverse).astype(jnp.bfloat16), v_ref[:end] * mask)
            context = context + dot_nn((far * inverse).astype(jnp.bfloat16), vr_ref[...] * mask)
            sums.append(highest + jnp.log(total))
        ctx_ref[start:end] = context.astype(jnp.bfloat16)
        lse_ref[start:end] = jnp.where(lane < HD, sums[0], sums[1])


def back_block(q_ref, g_ref, ctx_ref, lse_ref, keys, values, start, end, head, cut):
    mask = head_mask(head, jnp.bfloat16)
    queries = q_ref[start:end] * mask
    grads = g_ref[start:end] * mask
    inner = jnp.sum(
        grads.astype(jnp.float32) * ctx_ref[start:end].astype(jnp.float32), -1, keepdims=True
    )
    logsum = lse_ref[start:end, head * HD : head * HD + 1]
    probab = jnp.exp(cut(dot_nt(queries, keys) * FACTOR) - logsum)
    delta = (probab * (dot_nt(grads, values) - inner)).astype(jnp.bfloat16)
    return (
        dot_nn(delta, keys * mask) * FACTOR,
        dot_tn(delta, queries) * FACTOR,
        dot_tn(probab.astype(jnp.bfloat16), grads),
    )


def back_far_kernel(
    limit_ref, q_ref, g_ref, ctx_ref, lse_ref, kr_ref, vr_ref, dq_ref, dk_ref, dv_ref
):
    rows = q_ref.shape[0]
    step = row_step(rows)
    limit = limit_ref[0]
    dk = jnp.zeros(kr_ref.shape, jnp.float32)
    dv = jnp.zeros(kr_ref.shape, jnp.float32)
    for start in range(0, rows, step):
        end = start + step
        dq = jnp.zeros((step, LANES), jnp.float32)
        for head in range(2):
            one, two, three = back_block(
                q_ref, g_ref, ctx_ref, lse_ref, kr_ref[...], vr_ref[...], start, end, head,
                lambda s: before(s, limit),
            )
            dq, dk, dv = dq + one, dk + two, dv + three
        dq_ref[start:end] = dq
    dk_ref[...] = dk.astype(jnp.bfloat16)
    dv_ref[...] = dv.astype(jnp.bfloat16)


def back_own_kernel(
    q_ref, g_ref, ctx_ref, lse_ref, k_ref, v_ref, dqfar_ref, dq_ref, dk_ref, dv_ref
):
    rows = q_ref.shape[0]
    step = row_step(rows)
    dk_ref[...] = jnp.zeros(dk_ref.shape, jnp.float32)
    dv_ref[...] = jnp.zeros(dv_ref.shape, jnp.float32)
    for start in range(0, rows, step):
        end = start + step
        dq = dqfar_ref[start:end]
        for head in range(2):
            one, two, three = back_block(
                q_ref, g_ref, ctx_ref, lse_ref, k_ref[:end], v_ref[:end], start, end, head,
                lambda s: causal(s, start),
            )
            dq = dq + one
            dk_ref[:end] += two
            dv_ref[:end] += three
        dq_ref[start:end] = dq.astype(jnp.bfloat16)


def pair_spec(rows, base):
    return pl.BlockSpec((rows, LANES), lambda pair: (0, base + pair))


def cost(rows, keys, width, products):
    return pl.CostEstimate(
        flops=4 * 2 * products * rows * keys * width,
        bytes_accessed=2 * width * (4 * rows + 4 * keys),
        transcendentals=rows * keys * width // HD,
    )


LIMIT_SPEC = pl.BlockSpec(memory_space=pltpu.SMEM)
PARAMS = pltpu.CompilerParams(vmem_limit_bytes=VMEM_BYTES)


def attend(limit, queries, keyvals, far):
    rows, width = queries.shape
    extent = far.shape[0]
    pairs = width // LANES
    return pl.pallas_call(
        forward_kernel,
        grid=(pairs,),
        in_specs=[
            LIMIT_SPEC,
            pair_spec(rows, 0),
            pair_spec(rows, 0),
            pair_spec(rows, pairs),
            pair_spec(extent, 0),
            pair_spec(extent, pairs),
        ],
        out_specs=[pair_spec(rows, 0), pair_spec(rows, 0)],
        out_shape=[
            jax.ShapeDtypeStruct((rows, width), jnp.bfloat16),
            jax.ShapeDtypeStruct((rows, width), jnp.float32),
        ],
        compiler_params=PARAMS,
        cost_estimate=cost(rows, rows + extent, width, 2),
        name="attend",
    )(limit, queries, keyvals, keyvals, far, far)


def attend_back_far(limit, queries, grads, context, logsum, far):
    rows, width = queries.shape
    extent = far.shape[0]
    pairs = width // LANES
    return pl.pallas_call(
        back_far_kernel,
        grid=(pairs,),
        in_specs=[LIMIT_SPEC]
        + [pair_spec(rows, 0)] * 4
        + [pair_spec(extent, 0), pair_spec(extent, pairs)],
        out_specs=[pair_spec(rows, 0), pair_spec(extent, 0), pair_spec(extent, 0)],
        out_shape=[
            jax.ShapeDtypeStruct((rows, width), jnp.float32),
            jax.ShapeDtypeStruct((extent, width), jnp.bfloat16),
            jax.ShapeDtypeStruct((extent, width), jnp.bfloat16),
        ],
        compiler_params=PARAMS,
        cost_estimate=cost(rows, extent, width, 5),
        name="attend_back_far",
    )(limit, queries, grads, context, logsum, far, far)


def attend_back_own(queries, grads, context, logsum, keyvals, dq_far):
    rows, width = queries.shape
    pairs = width // LANES
    return pl.pallas_call(
        back_own_kernel,
        grid=(pairs,),
        in_specs=[pair_spec(rows, 0)] * 4
        + [pair_spec(rows, 0), pair_spec(rows, pairs), pair_spec(rows, 0)],
        out_specs=[pair_spec(rows, 0)] * 3,
        out_shape=[
            jax.ShapeDtypeStruct((rows, width), jnp.bfloat16),
            jax.ShapeDtypeStruct((rows, width), jnp.float32),
            jax.ShapeDtypeStruct((rows, width), jnp.float32),
        ],
        compiler_params=PARAMS,
        cost_estimate=cost(rows, rows, width, 5),
        name="attend_back_own",
    )(queries, grads, context, logsum, keyvals, keyvals, dq_far)


def pack_rows(pieces, rows):
    joined = jnp.concatenate(pieces, -1)
    spare = rows * LANES - joined.shape[-1]
    padded = jnp.pad(joined, ((0, 0), (0, spare)))
    return padded.reshape(joined.shape[0] * rows, LANES)


def unpack_rows(packed, shards, lengths):
    flat = packed.reshape(shards, -1)
    pieces, at = [], 0
    for length in lengths:
        pieces.append(flat[:, at : at + length].reshape(-1))
        at += length
    return pieces


def pick(blocks, index):
    return lax.dynamic_index_in_dim(blocks, index, 1, keepdims=False)


def swap_half(blocks, axis, pairs, mine):
    other = lax.ppermute(pick(blocks, 1 - mine), axis, pairs)
    total = pick(blocks, mine).astype(jnp.float32) + other.astype(jnp.float32)
    return total.astype(jnp.bfloat16)


def sum_cores(part, shards):
    blocks = part.reshape(shards // 2, 2, part.shape[0] // shards, part.shape[-1])
    core = lax.rem(lax.axis_index("dp"), 2)
    pairs = [(i, i + 1 - 2 * (i % 2)) for i in range(shards)]
    return swap_half(blocks, "dp", pairs, core)


def sum_ranks(held, ranks):
    if ranks != 2:
        return held
    blocks = held.reshape(held.shape[0], 2, held.shape[1] // 2, held.shape[2])
    return swap_half(blocks, "seq", [(0, 1), (1, 0)], lax.axis_index("seq"))


def sum_chips(held, shards):
    return lax.psum_scatter(
        held.reshape(-1, held.shape[-1]),
        "dp",
        scatter_dimension=0,
        axis_index_groups=[list(range(0, shards, 2)), list(range(1, shards, 2))],
        tiled=True,
    )


def finish_sum(owned, ranks, seq_first):
    if ranks != 2:
        return lax.psum(owned, "seq").astype(jnp.float32)
    other = lax.ppermute(owned, "seq", [(0, 1), (1, 0)])
    if not seq_first:
        return owned.astype(jnp.float32) + other.astype(jnp.float32)
    first = lax.axis_index("seq") == 0
    top = jnp.where(first, owned, other)
    bottom = jnp.where(first, other, owned)
    return jnp.concatenate([top, bottom], 0).astype(jnp.float32)


def local(
    block_entry_tokens,
    result_cotangent,
    leading_scale_factor,
    leading_bias_vector,
    query_key_value_matrix,
    query_key_value_bias,
    attention_exit_matrix,
    attention_exit_bias,
    latter_scale_factor,
    latter_bias_vector,
    expand_projection_matrix,
    expand_projection_offset,
    contract_projection_matrix,
    contract_projection_offset,
    shards,
    ranks,
):
    f32, bf16 = jnp.float32, jnp.bfloat16
    hidden = block_entry_tokens.reshape(-1, block_entry_tokens.shape[-1]).astype(f32)
    tokens, width = hidden.shape
    place = lax.axis_index("seq")
    limit = (place * tokens).astype(jnp.int32).reshape(1)
    vectors = (
        leading_scale_factor,
        leading_bias_vector,
        query_key_value_bias,
        attention_exit_bias,
        latter_scale_factor,
        latter_bias_vector,
        expand_projection_offset,
        contract_projection_offset,
    )
    lengths = [vector.shape[0] for vector in vectors]
    rows = query_key_value_matrix.shape[0]
    small = pack_rows([vector[None] for vector in vectors], rows)
    attn_whole = lax.all_gather(
        jnp.concatenate([query_key_value_matrix, attention_exit_matrix, small], 1),
        "dp",
        axis=0,
        tiled=True,
    )
    w_up = lax.all_gather(expand_projection_matrix, "dp", axis=0, tiled=True)
    w_down = lax.all_gather(contract_projection_matrix, "dp", axis=0, tiled=True)
    w_q = attn_whole[:, :width]
    w_kv = attn_whole[:, width : 3 * width]
    w_qkv = attn_whole[:, : 3 * width]
    w_out = attn_whole[:, 3 * width : 4 * width]
    gain_one, shift_one, b_qkv, b_out, gain_two, shift_two, b_up, b_down = (
        vector.astype(f32) for vector in unpack_rows(attn_whole[:, 4 * width :], shards, lengths)
    )

    normed_one, pull_one = jax.vjp(standardize_features, hidden, gain_one, shift_one)
    h_one = normed_one.astype(bf16)
    keyvals = (dot_nn(h_one, w_kv) + b_qkv[width:]).astype(bf16)
    if ranks == 2:
        far = lax.ppermute(keyvals, "seq", [(0, 1)])
    else:
        far = lax.all_gather(keyvals, "seq", axis=0, tiled=True)
    queries = (dot_nn(h_one, w_q) + b_qkv[:width]).astype(bf16)
    context, logsum = attend(limit, queries, keyvals, far)
    resid = hidden + dot_nn(context, w_out) + b_out

    normed_two, pull_two = jax.vjp(standardize_features, resid, gain_two, shift_two)
    h_two = normed_two.astype(bf16)
    upact = dot_nn(h_two, w_up) + b_up
    activ, gelu_pull = jax.vjp(gelu_apply, upact)
    act_low = activ.astype(bf16)
    out_delta = result_cotangent.reshape(tokens, width)
    down_part = dot_tn(act_low, out_delta).astype(bf16)
    down_held = sum_cores(down_part, shards)
    down_held, act_low, out_delta = lax.optimization_barrier((down_held, act_low, out_delta))
    down_held = sum_ranks(down_held, ranks)
    out_float = out_delta.astype(f32)
    downshift_grad = jnp.sum(out_float, 0)
    up_delta = gelu_pull(dot_nt(out_delta, w_down))[0].astype(bf16)
    upshift_grad = jnp.sum(up_delta.astype(f32), 0)
    up_part = dot_tn(h_two, up_delta).astype(bf16)
    up_part, up_delta, down_held = lax.optimization_barrier((up_part, up_delta, down_held))
    down_owned = sum_chips(down_held, shards)
    up_held = sum_cores(up_part, shards)
    output = resid + dot_nn(act_low, w_down) + b_down
    norm_two_delta = dot_nt(up_delta, w_up)
    resid_part, midgain_grad, midshift_grad = pull_two(norm_two_delta)
    resid_grad = out_float + resid_part
    proj_delta = resid_grad.astype(bf16)
    outshift_grad = jnp.sum(proj_delta.astype(f32), 0)
    ctx_delta = dot_nt(proj_delta, w_out).astype(bf16)
    dq_far, dk_far, dv_far = attend_back_far(limit, queries, ctx_delta, context, logsum, far)
    if ranks == 2:
        dk_back = lax.ppermute(dk_far, "seq", [(1, 0)])
        dv_back = lax.ppermute(dv_far, "seq", [(1, 0)])
    else:
        dk_back = lax.psum_scatter(dk_far, "seq", scatter_dimension=0, tiled=True)
        dv_back = lax.psum_scatter(dv_far, "seq", scatter_dimension=0, tiled=True)
    up_held, dq_far = lax.optimization_barrier((up_held, dq_far))
    up_owned = sum_chips(up_held, shards)
    dq, dk_own, dv_own = attend_back_own(queries, ctx_delta, context, logsum, keyvals, dq_far)
    out_part = dot_tn(context, proj_delta).astype(bf16)
    down_owned, dq, dk_own, dv_own = lax.optimization_barrier((down_owned, dq, dk_own, dv_own))
    qkv_delta = jnp.concatenate(
        [
            dq,
            (dk_own + dk_back.astype(f32)).astype(bf16),
            (dv_own + dv_back.astype(f32)).astype(bf16),
        ],
        1,
    )
    qkvshift_grad = jnp.sum(qkv_delta.astype(f32), 0)
    qkv_part = dot_tn(h_one, qkv_delta).astype(bf16)
    input_portion, prenorm_gain_gradient, prenorm_shift_gradient = pull_one(
        dot_nt(qkv_delta, w_qkv)
    )
    input_grad = resid_grad + input_portion
    small_parts = (
        prenorm_gain_gradient,
        prenorm_shift_gradient,
        qkvshift_grad,
        outshift_grad,
        midgain_grad,
        midshift_grad,
        upshift_grad,
        downshift_grad,
    )
    small_part = pack_rows(
        [part.astype(bf16).reshape(shards, -1) for part in small_parts], rows
    )
    attn_held = sum_cores(jnp.concatenate([qkv_part, out_part, small_part], 1), shards)
    up_owned, attn_held = lax.optimization_barrier((up_owned, attn_held))
    attn_held = sum_ranks(attn_held, ranks)
    attn_owned = sum_chips(attn_held, shards)
    upmatrix_grad = finish_sum(up_owned, ranks, False)
    downmatrix_grad = finish_sum(down_owned, ranks, True)
    attn_sum = finish_sum(attn_owned, ranks, True)
    gain_g, shift_g, qkvshift, outshift, midgain, midshift, upshift, downshift = unpack_rows(
        attn_sum[:, 4 * width :], 1, lengths
    )
    return (
        output.reshape(1, tokens, width),
        input_grad.reshape(1, tokens, width),
        gain_g,
        shift_g,
        attn_sum[:, : 3 * width],
        qkvshift,
        attn_sum[:, 3 * width : 4 * width],
        outshift,
        midgain,
        midshift,
        upmatrix_grad,
        upshift,
        downmatrix_grad,
        downshift,
    )


def solution(mesh):
    in_specs = (
        P("dp", "seq", None),
        P("dp", "seq", None),
        P("dp"),
        P("dp"),
        P("dp", None),
        P("dp"),
        P("dp", None),
        P("dp"),
        P("dp"),
        P("dp"),
        P("dp", None),
        P("dp"),
        P("dp", None),
        P("dp"),
    )
    out_specs = (
        P("dp", "seq", None),
        P("dp", "seq", None),
        P("dp"),
        P("dp"),
        P("dp", None),
        P("dp"),
        P("dp", None),
        P("dp"),
        P("dp"),
        P("dp"),
        P("dp", None),
        P("dp"),
        P("dp", None),
        P("dp"),
    )
    body = functools.partial(local, shards=mesh.shape["dp"], ranks=mesh.shape["seq"])
    return jax.shard_map(body, mesh=mesh, in_specs=in_specs, out_specs=out_specs, check_vma=False)
```
